512 devices in a mesh: ctx: 64 (over z_lo, y, core), head: 8 (over z_hi, x).
Axes of the slice: x: 4, y: 8, z: 8 (z_hi: 2, z_lo: 4; z = z_hi * 4 + z_lo), core: 2. Of those that a mesh axis runs over, the one named last changes fastest.
Arguments:
- queries: bfloat16 [8192, 4096], P('ctx', 'head'), may hold values from -4.5 to 4.5
- key_states: bfloat16 [8192, 4096], P('ctx', 'head'), may hold values from -4.5 to 4.5
- values: bfloat16 [8192, 4096], P('ctx', 'head'), may hold values from -6 to 6
- out_grad: bfloat16 [8192, 4096], P(('ctx', 'head')), may hold values from -6 to 6
- pattern: int32 [64, 3], replicated, may hold values from 0 to 63, as said below
- global_ids: int32 [2], replicated, may hold values from 0 to 63, as said below
Outputs:
- query_grad: bfloat16 [8192, 4096], P('ctx', 'head')
- key_grad: bfloat16 [8192, 4096], P('ctx', 'head')
- value_grad: bfloat16 [8192, 4096], P('ctx', 'head')
The draws below stay inside these ranges and needn't reach their ends.
Inputs may be any that keep to these rules, and one draw needn't show every extreme that they name: Each pattern[b, r] is a block of the context shard of query block b or of one of the two shards beside it on the circular sequence: pattern[b, r] - b is -1, 0 or 1 modulo 64. `global_ids`: 2 different blocks; the last entry is the sequence's last block, 63.
All inputs are finite; a program needn't handle non-finite values.
Results may differ from the reference program's by a relative error of at most 0.009.
Values may be sent and summed in bfloat16 or wider, within the bound.
A program may use at most 64 MiB of HBM per device.

```python
import math
import jax
import jax.numpy as jnp
from jax import lax

HD = 128
BLK = 128
RND = 3
GLB = 2
D = 4096
QB_DEV = 1
TOKENS = 8192
NBLK = 64


def draw_queries(key, part):
    key = jax.random.fold_in(key, 11)
    return jnp.clip(jax.random.normal(key, (TOKENS, D), jnp.float32), -4.5, 4.5).astype(jnp.bfloat16)


def draw_key_states(key, part):
    key = jax.random.fold_in(key, 12)
    return jnp.clip(jax.random.normal(key, (TOKENS, D), jnp.float32), -4.5, 4.5).astype(jnp.bfloat16)


def draw_pattern(key, part):
    key = jax.random.fold_in(key, 21)
    shards = NBLK // QB_DEV
    blocks = jnp.arange(NBLK, dtype=jnp.int32)[:, None]
    step_key, slot_key = jax.random.split(key)
    offsets = jax.random.randint(step_key, (NBLK, RND), -1, 2)
    within = jax.random.randint(slot_key, (NBLK, RND), 0, QB_DEV)
    owner_shard = (blocks // QB_DEV + offsets) % shards
    return (owner_shard * QB_DEV + within).astype(jnp.int32)


def draw_global_ids(key, part):
    key = jax.random.fold_in(key, 31)
    others = jax.random.permutation(key, NBLK - 1)[:GLB - 1].astype(jnp.int32)
    last_block = jnp.full((1,), NBLK - 1, jnp.int32)
    return jnp.concatenate([others, last_block]).astype(jnp.int32)


def block_levels(rng, shape, cuts, least, high):
    def one(dim, shards_of):
        heights = jax.random.uniform(jax.random.fold_in(jax.random.fold_in(rng, 6), dim), (shards_of,), jnp.float32, least / len(cuts), high / len(cuts))
        return jnp.repeat(jnp.exp(heights), shape[dim] // shards_of).reshape((-1,) + (1,) * (len(shape) - dim - 1))

    factor_of = one(*cuts[0])
    for cut in cuts[1:]:
        factor_of = factor_of * one(*cut)
    return factor_of


def gaussian(key, dims, scale, reach, cuts=(), kind=jnp.bfloat16):
    loudness = block_levels(key, dims, cuts, -0.22, 0.18) if cuts else 1.0
    drawn = jax.random.normal(key, dims, jnp.float32) * scale * loudness
    return jnp.minimum(jnp.maximum(drawn, -reach), reach).astype(kind)


def setup_inputs(seed: int = 0) -> dict:
    key_of = jax.random.split(jax.random.key(seed), 7)
    return {
        "queries": draw_queries(jax.random.fold_in(key_of[6], 71), 0),
        "key_states": draw_key_states(jax.random.fold_in(key_of[6], 71), 0),
        "values": gaussian(key_of[2], (TOKENS, D), 1.0, 6.0, ((0, 64), (1, 8))),
        "out_grad": gaussian(key_of[3], (TOKENS, D), 1.0, 6.0, ((0, 512),)),
        "pattern": draw_pattern(jax.random.fold_in(key_of[6], 71), 0),
        "global_ids": draw_global_ids(jax.random.fold_in(key_of[6], 71), 0),
    }


def entry_table(pattern, global_ids):
    block_total = pattern.shape[0]
    block_ids = jnp.arange(block_total, dtype=jnp.int32)
    local_ids = jnp.stack([(block_ids - 1) % block_total, block_ids, (block_ids + 1) % block_total], axis=1)
    global_cols = jnp.broadcast_to(global_ids.astype(jnp.int32)[None, :], (block_total, global_ids.shape[0]))
    return jnp.concatenate([local_ids, global_cols, pattern.astype(jnp.int32)], axis=1).astype(jnp.int32)

def reference(queries, key_states, values, out_grad, pattern, global_ids):
    tok_total, feat_width = queries.shape
    head_count = feat_width // HD
    block_total = tok_total // BLK
    score_scale = 1.0 / math.sqrt(HD)
    entry_lists = entry_table(pattern, global_ids)
    query_blocks = queries.reshape(block_total, BLK, head_count, HD)
    key_blocks = key_states.reshape(block_total, BLK, head_count, HD)
    value_blocks = values.reshape(block_total, BLK, head_count, HD)
    grad_blocks = out_grad.reshape(block_total, BLK, head_count, HD)

    def one_block(block_num, state_now):
        query_acc, key_acc, value_acc = state_now
        entry_ids = entry_lists[block_num]
        query_f = query_blocks[block_num].astype(jnp.float32)
        grad_f = grad_blocks[block_num].astype(jnp.float32)
        key_f = key_blocks[entry_ids].astype(jnp.float32)
        value_f = value_blocks[entry_ids].astype(jnp.float32)
        scores = jnp.einsum('ihd,ejhd->hiej', query_f, key_f) * score_scale
        row_top = lax.optimization_barrier(jnp.max(scores, axis=(2, 3), keepdims=True))
        log_total = row_top + jnp.log(lax.optimization_barrier(jnp.sum(jnp.exp(scores - row_top), axis=(2, 3), keepdims=True)))
        prob_full = jnp.exp(scores - log_total)
        dprobs = jnp.einsum('ihd,ejhd->hiej', grad_f, value_f)
        deltas = lax.optimization_barrier(jnp.sum(prob_full * dprobs, axis=(2, 3), keepdims=True))
        score_grad = (prob_full * (dprobs - deltas) * score_scale).astype(jnp.bfloat16)
        prob_low = prob_full.astype(jnp.bfloat16)
        score_grad, prob_low = lax.optimization_barrier((score_grad, prob_low))
        score_grad = score_grad.astype(jnp.float32)
        prob_low = prob_low.astype(jnp.float32)
        query_acc = query_acc.at[block_num].set(jnp.einsum('hiej,ejhd->ihd', score_grad, key_f))
        key_acc = key_acc.at[entry_ids].add(jnp.einsum('hiej,ihd->ejhd', score_grad, query_f))
        value_acc = value_acc.at[entry_ids].add(jnp.einsum('hiej,ihd->ejhd', prob_low, grad_f))
        return (query_acc, key_acc, value_acc)
    zeros_acc = jnp.zeros((block_total, BLK, head_count, HD), jnp.float32)
    query_acc, key_acc, value_acc = lax.fori_loop(0, block_total, one_block, (zeros_acc, zeros_acc, zeros_acc))
    return (query_acc.reshape(tok_total, feat_width).astype(jnp.bfloat16), key_acc.reshape(tok_total, feat_width).astype(jnp.bfloat16), value_acc.reshape(tok_total, feat_width).astype(jnp.bfloat16))
```

```python
import functools
import math

import jax
import jax.numpy as jnp
from jax import lax
from jax.experimental import pallas as pl
from jax.experimental.pallas import tpu as pltpu
from jax.sharding import PartitionSpec as P

HD = 128
BLK = 128
SCALE = 1.0 / math.sqrt(HD)
MESH = pl.DeviceIdType.MESH
BF = jnp.bfloat16
F32 = jnp.float32
NT = (((1,), (1,)), ((), ()))
NN = (((1,), (0,)), ((), ()))
TN = (((0,), (0,)), ((), ()))


def dot(a, b, dims):
    return lax.dot_general(a, b, dims, preferred_element_type=F32)


def kernel(
    pat, gid, q_ref, k_ref, v_ref, g_ref, dq_ref, dk_ref, dv_ref,
    q2, kv2, kvn, do2, cand, rsel, hold, gkv, gpart, rgr, hsum, gs0, gs63,
    nbo, nbi, own, fin, dqb, el, dpl, dsg,
    in_sem, pair_s, pair_r, nb_s, nb_r, do_s, do_r, sel_s, sel_r, sc_s, sc_r,
    ag_s, ag_r, rg_s, rg_r, gs_s, gs_r, gn_s, gn_r, out_l, out_s, out_r,
):
    me = lax.axis_index("ctx")
    head = lax.axis_index("head")
    core = me % 2
    chip = me // 2
    y = chip % 8
    z = chip // 8
    sib = {"ctx": chip * 2 + 1 - core}
    left = {"ctx": (me + 62) % 64}
    right = {"ctx": (me + 2) % 64}
    mine = pl.multiple_of(core * 256, 256)
    theirs = pl.multiple_of((1 - core) * 256, 256)

    def remote(src, dst, ss, rs, dev):
        return pltpu.make_async_remote_copy(
            src_ref=src, dst_ref=dst, send_sem=ss, recv_sem=rs,
            device_id=dev, device_id_type=MESH,
        )

    def local(src, dst, sem):
        return pltpu.make_async_copy(src, dst, sem)

    def wait(ref, sem):
        pltpu.make_async_copy(ref, ref, sem).wait()

    def far_y(i):
        return (y + 4 + (1 - 2 * (i % 2)) * ((i + 1) // 2)) % 8

    def plane(t):
        ty = far_y(t // 4)
        tz = (z + 3 - t % 4) % 4
        return ty, tz, {"ctx": (tz * 8 + ty) * 2 + core}

    def group(t):
        th = (head + 7 - t // 2) % 8
        tc = (core + 1 - t % 2) % 2
        return th, tc, {"ctx": chip * 2 + tc, "head": th}

    loads = [
        local(k_ref.at[:, pl.ds(mine, 256)], kv2.at[core, :, pl.ds(0, 256)], in_sem.at[0]),
        local(v_ref.at[:, pl.ds(mine, 256)], kv2.at[core, :, pl.ds(256, 256)], in_sem.at[1]),
        local(q_ref.at[:, pl.ds(mine, 256)], q2.at[core], in_sem.at[2]),
    ]
    for cp in loads:
        cp.start()

    bar = pltpu.get_barrier_semaphore()

    @pl.loop(0, 31)
    def _(t):
        pl.semaphore_signal(bar, inc=1, device_id=plane(t)[2], device_id_type=MESH)

    @pl.loop(0, 15)
    def _(t):
        pl.semaphore_signal(bar, inc=1, device_id=group(t)[2], device_id_type=MESH)

    pl.semaphore_wait(bar, 46)

    pairs = [
        remote(k_ref.at[:, pl.ds(theirs, 256)], kv2.at[core, :, pl.ds(0, 256)], pair_s.at[0], pair_r.at[0], sib),
        remote(v_ref.at[:, pl.ds(theirs, 256)], kv2.at[core, :, pl.ds(256, 256)], pair_s.at[1], pair_r.at[1], sib),
        remote(q_ref.at[:, pl.ds(theirs, 256)], q2.at[core], pair_s.at[2], pair_r.at[2], sib),
    ]
    for cp in pairs:
        cp.start()
    loads[0].wait()
    loads[1].wait()
    pairs[0].wait_recv()
    pairs[1].wait_recv()

    def piece(ref, tz, ty):
        return ref.at[pl.ds(pl.multiple_of(ty * 16, 16), 16), pl.ds(pl.multiple_of(tz * 128, 128), 128)]

    @pl.when(chip == 31)
    def _():
        @pl.loop(0, 31)
        def _(t):
            ty, tz, dev = plane(t)
            remote(piece(kv2.at[1], tz, ty), hold.at[1], sc_s, sc_r, dev).start()

        local(piece(kv2.at[1], z, y), hold.at[1], sc_r).start()

    g0 = gid[0]
    cand[...] = kv2[g0 % 2]

    @pl.loop(0, 31)
    def _(t):
        ty, tz, dev = plane(t)
        remote(piece(cand, tz, ty), rsel.at[chip], sel_s, sel_r, dev).start()

    local(piece(cand, z, y), rsel.at[chip], sel_r).start()

    nbk = [
        remote(kv2.at[1], kvn.at[0], nb_s.at[0], nb_r.at[0], right),
        remote(kv2.at[0], kvn.at[1], nb_s.at[1], nb_r.at[1], left),
    ]
    for cp in nbk:
        cp.start()

    rows = pl.ds(pl.multiple_of(head * 16, 16), 16)

    def gcols(th, tc):
        return pl.ds(pl.multiple_of(th * 512 + tc * 256, 256), 256)

    @pl.loop(0, 15)
    def _(t):
        th, tc, dev = group(t)
        remote(g_ref.at[:, gcols(th, tc)], do2.at[core, rows], do_s, do_r, dev).start()

    local(g_ref.at[:, gcols(head, core)], do2.at[core, rows], do_r).start()

    def spread(g):
        @pl.loop(0, 31)
        def _(t):
            _, _, dev = plane(t)
            remote(hold.at[g], piece(gkv.at[g], z, y), ag_s.at[g], ag_r.at[g], dev).start()

        local(hold.at[g], piece(gkv.at[g], z, y), ag_r.at[g]).start()

    wait(hold.at[1], sc_r)
    spread(1)
    wait(rsel, sel_r)
    hold[0] = rsel[g0 // 2]
    spread(0)

    loads[2].wait()
    pairs[2].wait_recv()
    nbk[0].wait_recv()
    nbk[1].wait_recv()
    wait(do2, do_r)

    def count(block, target):
        n = jnp.int32(1)
        for r in range(3):
            n = n + jnp.where(pat[block, r] == target, 1, 0)
        return n.astype(F32)

    b0, b1 = chip * 2, chip * 2 + 1
    bl, br = (b0 + 63) % 64, (b0 + 2) % 64
    lane = lax.broadcasted_iota(jnp.int32, (1, 256), 1) < 128
    mult = [
        jnp.where(lane, count(b0, bl), count(b1, br)),
        jnp.where(lane, count(b0, b0), count(b1, b0)),
        jnp.where(lane, count(b0, b1), count(b1, b1)),
    ]

    def cols(hh):
        return slice(hh * 128, hh * 128 + 128), slice(256 + hh * 128, 384 + hh * 128)

    stats = []
    for hh in range(2):
        kc, vc = cols(hh)
        qh = q2[:, :, kc].reshape(256, 128)
        gh = do2[:, :, kc].reshape(256, 128)
        s_out = jnp.concatenate([dot(kvn[0, :, kc], qh[:128], NT), dot(kvn[1, :, kc], qh[128:], NT)], axis=1) * SCALE
        s_in = dot(kv2[:, :, kc].reshape(256, 128), qh, NT) * SCALE
        top = jnp.maximum(jnp.max(s_out, axis=0, keepdims=True), jnp.max(s_in, axis=0, keepdims=True))
        e_out = jnp.exp(s_out - top) * mult[0]
        e_a = jnp.exp(s_in[:128] - top) * mult[1]
        e_b = jnp.exp(s_in[128:] - top) * mult[2]
        d_out = jnp.concatenate([dot(kvn[0, :, vc], gh[:128], NT), dot(kvn[1, :, vc], gh[128:], NT)], axis=1)
        d_in = dot(kv2[:, :, vc].reshape(256, 128), gh, NT)
        total = jnp.sum(e_out + e_a + e_b, axis=0, keepdims=True)
        dsum = jnp.sum(e_out * d_out + e_a * d_in[:128] + e_b * d_in[128:], axis=0, keepdims=True)
        el[hh, 0:128] = e_out
        el[hh, 128:256] = e_a
        el[hh, 256:384] = e_b
        dpl[hh, 0:128] = d_out
        dpl[hh, 128:384] = d_in
        stats.append((top, total, dsum))

    wait(gkv.at[1], ag_r.at[1])
    wait(gkv.at[0], ag_r.at[0])
    rowf = []
    for hh in range(2):
        kc, vc = cols(hh)
        top_l, total_l, dsum_l = stats[hh]
        qh = q2[:, :, kc].reshape(256, 128)
        gh = do2[:, :, kc].reshape(256, 128)
        s = dot(gkv[:, :, kc].reshape(256, 128), qh, NT) * SCALE
        dp = dot(gkv[:, :, vc].reshape(256, 128), gh, NT)
        top = jnp.maximum(top_l, jnp.max(s, axis=0, keepdims=True))
        e = jnp.exp(s - top)
        scale_l = jnp.exp(top_l - top)
        inv = 1.0 / (total_l * scale_l + jnp.sum(e, axis=0, keepdims=True))
        delta = (dsum_l * scale_l + jnp.sum(e * dp, axis=0, keepdims=True)) * inv
        p = e * inv
        ds = (p * (dp - delta) * SCALE).astype(BF)
        dsg[hh] = ds
        gpart[:, :, kc] = dot(ds, qh, NN).astype(BF).reshape(2, 128, 128)
        gpart[:, :, vc] = dot(p.astype(BF), gh, NN).astype(BF).reshape(2, 128, 128)
        rowf.append((scale_l * inv, delta))

        @pl.loop(0, 16)
        def _(t):
            ty = far_y(t // 2)
            tz = hh + 2 * (t % 2)
            src = gpart.at[:, pl.ds(pl.multiple_of(ty * 16, 16), 16), pl.ds(pl.multiple_of(tz * 128, 128), 128)]
            self_piece = jnp.logical_and(ty == y, tz == z)

            @pl.when(self_piece)
            def _():
                local(src, rgr.at[chip], rg_r).start()

            @pl.when(jnp.logical_not(self_piece))
            def _():
                remote(src, rgr.at[chip], rg_s, rg_r, {"ctx": (tz * 8 + ty) * 2 + core}).start()

    nbg = []
    for hh in range(2):
        kc, vc = cols(hh)
        qh = q2[:, :, kc].reshape(256, 128)
        gh = do2[:, :, kc].reshape(256, 128)
        rf, delta = rowf[hh]
        p0 = el[hh, 0:128] * rf
        ds0 = (p0 * (dpl[hh, 0:128] - delta) * SCALE).astype(BF)
        p0 = p0.astype(BF)
        nbo[0, hh, :, 0:128] = dot(ds0[:, :128], qh[:128], NN).astype(BF)
        nbo[0, hh, :, 128:256] = dot(p0[:, :128], gh[:128], NN).astype(BF)
        nbo[1, hh, :, 0:128] = dot(ds0[:, 128:], qh[128:], NN).astype(BF)
        nbo[1, hh, :, 128:256] = dot(p0[:, 128:], gh[128:], NN).astype(BF)
        for side, dev in ((0, left), (1, right)):
            cp = remote(nbo.at[side, hh], nbi.at[1 - side, hh], gn_s.at[side, hh], gn_r.at[1 - side, hh], dev)
            cp.start()
            nbg.append(cp)
        p1 = el[hh, 128:384] * rf
        ds1 = (p1 * (dpl[hh, 128:384] - delta) * SCALE).astype(BF)
        own[:, :, kc] = dot(ds1, qh, NN).reshape(2, 128, 128)
        own[:, :, vc] = dot(p1.astype(BF), gh, NN).reshape(2, 128, 128)
        dq = dot(ds1, kv2[:, :, kc].reshape(256, 128), TN)
        dq = dq + dot(dsg[hh], gkv[:, :, kc].reshape(256, 128), TN)
        dqb[0, :, kc] = (dq[:128] + dot(ds0[:, :128], kvn[0, :, kc], TN)).astype(BF)
        dqb[1, :, kc] = (dq[128:] + dot(ds0[:, 128:], kvn[1, :, kc], TN)).astype(BF)

    my_cols = pl.ds(mine, 256)
    outs = [
        remote(dqb.at[1 - core], dq_ref.at[:, my_cols], out_s.at[0], out_r.at[0], sib),
        local(dqb.at[core], dq_ref.at[:, my_cols], out_l.at[0]),
    ]
    for cp in outs:
        cp.start()

    wait(rgr, rg_r)
    acc = rgr[0].astype(F32)
    for j in range(1, 32):
        acc = acc + rgr[j].astype(F32)
    hsum[...] = acc.astype(BF)

    @pl.loop(0, 31)
    def _(t):
        _, _, dev = plane(t)
        remote(hsum.at[0], piece(gs0, z, y), gs_s.at[0], gs_r.at[0], dev).start()

    local(hsum.at[0], piece(gs0, z, y), gs_r.at[0]).start()

    @pl.when(chip == 31)
    def _():
        local(hsum.at[1], piece(gs63, z, y), gs_r.at[1]).start()

    @pl.when(chip != 31)
    def _():
        remote(hsum.at[1], piece(gs63, z, y), gs_s.at[1], gs_r.at[1], {"ctx": 62 + core}).start()

    for cp in nbg:
        cp.wait_recv()
    for b in range(2):
        for hh in range(2):
            kc, vc = cols(hh)
            own[b, :, kc] += nbi[b, hh, :, 0:128].astype(F32)
            own[b, :, vc] += nbi[b, hh, :, 128:256].astype(F32)

    @pl.when(chip == 31)
    def _():
        wait(gs63, gs_r.at[1])
        own[1] += gs63[...].astype(F32)

    wait(gs0, gs_r.at[0])
    for b in range(2):
        pick = jnp.where(g0 == b0 + b, 1.0, 0.0).astype(F32)
        fin[b] = (own[b] + gs0[...].astype(F32) * pick).astype(BF)

    lo, hi = pl.ds(0, 256), pl.ds(256, 256)
    more = [
        remote(fin.at[1 - core, :, lo], dk_ref.at[:, my_cols], out_s.at[1], out_r.at[1], sib),
        remote(fin.at[1 - core, :, hi], dv_ref.at[:, my_cols], out_s.at[2], out_r.at[2], sib),
        local(fin.at[core, :, lo], dk_ref.at[:, my_cols], out_l.at[1]),
        local(fin.at[core, :, hi], dv_ref.at[:, my_cols], out_l.at[2]),
    ]
    for cp in more:
        cp.start()

    for cp in pairs:
        cp.wait_send()
    for cp in nbk:
        cp.wait_send()
    for cp in nbg:
        cp.wait_send()

    @pl.when(chip == 31)
    def _():
        wait(rsel.at[pl.ds(0, 31)], sc_s)

    @pl.when(chip != 31)
    def _():
        wait(hsum.at[1], gs_s.at[1])

    wait(rsel.at[pl.ds(0, 31)], sel_s)
    wait(rsel.at[pl.ds(0, 30)], do_s)
    wait(rsel.at[pl.ds(0, 31)], ag_s.at[0])
    wait(rsel.at[pl.ds(0, 31)], ag_s.at[1])
    wait(rgr.at[pl.ds(0, 31)], rg_s)
    wait(rsel.at[pl.ds(0, 31)], gs_s.at[0])
    for cp in outs + more:
        cp.wait()


def shards(queries, key_states, values, out_grad, pattern, global_ids):
    vmem = pltpu.VMEM
    dma = pltpu.SemaphoreType.DMA
    anyspace = pl.BlockSpec(memory_space=pl.ANY)
    smem = pl.BlockSpec(memory_space=pltpu.SMEM)
    out = jax.ShapeDtypeStruct((BLK, 512), BF)
    return pl.pallas_call(
        kernel,
        out_shape=(out, out, out),
        in_specs=[smem, smem, anyspace, anyspace, anyspace, anyspace],
        out_specs=(anyspace, anyspace, anyspace),
        scratch_shapes=[
            vmem((2, BLK, 256), BF),
            vmem((2, BLK, 512), BF),
            vmem((2, BLK, 512), BF),
            vmem((2, BLK, 256), BF),
            vmem((BLK, 512), BF),
            vmem((32, 16, 128), BF),
            vmem((2, 16, 128), BF),
            vmem((2, BLK, 512), BF),
            vmem((2, BLK, 512), BF),
            vmem((32, 2, 16, 128), BF),
            vmem((2, 16, 128), BF),
            vmem((BLK, 512), BF),
            vmem((BLK, 512), BF),
            vmem((2, 2, BLK, 256), BF),
            vmem((2, 2, BLK, 256), BF),
            vmem((2, BLK, 512), F32),
            vmem((2, BLK, 512), BF),
            vmem((2, BLK, 256), BF),
            vmem((2, 384, 256), F32),
            vmem((2, 384, 256), F32),
            vmem((2, 256, 256), BF),
            dma((3,)),
            dma((3,)), dma((3,)),
            dma((2,)), dma((2,)),
            dma, dma,
            dma, dma,
            dma, dma,
            dma((2,)), dma((2,)),
            dma, dma,
            dma((2,)), dma((2,)),
            dma((2, 2)), dma((2, 2)),
            dma((3,)), dma((3,)), dma((3,)),
        ],
        name="block_attention_grads",
        compiler_params=pltpu.CompilerParams(
            collective_id=0, has_side_effects=True, vmem_limit_bytes=32 * 1024 * 1024
        ),
    )(pattern, global_ids, queries, key_states, values, out_grad)


def solution(mesh):
    placed = (
        P("ctx", "head"),
        P("ctx", "head"),
        P("ctx", "head"),
        P(("ctx", "head"), None),
        P(),
        P(),
    )
    return jax.shard_map(
        shards,
        mesh=mesh,
        in_specs=placed,
        out_specs=(P("ctx", "head"), P("ctx", "head"), P("ctx", "head")),
        check_vma=False,
    )
```

```python
import functools
import math

import jax
import jax.numpy as jnp
from jax import lax
from jax.experimental import pallas as pl
from jax.experimental.pallas import tpu as pltpu
from jax.sharding import PartitionSpec as P

HD = 128
BLK = 128
SCALE = 1.0 / math.sqrt(HD)
MESH = pl.DeviceIdType.MESH
BF = jnp.bfloat16
F32 = jnp.float32
NT = (((1,), (1,)), ((), ()))
NN = (((1,), (0,)), ((), ()))
TN = (((0,), (0,)), ((), ()))


def remote(src, dst, ss, rs, dev):
    return pltpu.make_async_remote_copy(
        src_ref=src, dst_ref=dst, send_sem=ss, recv_sem=rs,
        device_id=dev, device_id_type=MESH,
    )


def local(src, dst, sem):
    return pltpu.make_async_copy(src, dst, sem)


def wait(ref, sem):
    pltpu.make_async_copy(ref, ref, sem).wait()


def signal(sem, dev):
    pl.semaphore_signal(sem, inc=1, device_id=dev, device_id_type=MESH)


def dot(a, b, dims):
    return lax.dot_general(a, b, dims, preferred_element_type=F32)


def kernel(
    pat_ref, gid_ref, q_ref, k_ref, v_ref, g_ref, all_ref,
    pat, gid, q2, kv2, kvn, do2, cand, rsel, hold, gkv, gpart, rgr, hsum, gs0, gs63,
    nbo, nbi, own, fin, dqb, el, dpl, dsg,
    ok_sib, ok_group, ok_plane, in_sem, pair_s, pair_r, nb_s, nb_r, do_s, do_r, sel_s, sel_r, sc_s, sc_r,
    ag_s, ag_r, rg_s, rg_r, gs_s, gs_r, gn_s, gn_r, out_l, out_s, out_r,
):
    me = lax.axis_index("ctx")
    head = lax.axis_index("head")
    core = me % 2
    chip = me // 2
    y = chip % 8
    z = chip // 8
    sib = {"ctx": chip * 2 + 1 - core}
    left = {"ctx": (me + 62) % 64}
    right = {"ctx": (me + 2) % 64}
    mine = pl.multiple_of(core * 256, 256)
    theirs = pl.multiple_of((1 - core) * 256, 256)

    def around(base, step, size):
        return jnp.where(base + step >= size, base + step - size, base + step)

    ys = [around(y, d, 8) for d in range(8)]
    zs = [around(z, d, 4) for d in range(4)]
    plane = []
    for dy in (4, 3, 5, 2, 6, 1, 7, 0):
        for dz in (3, 2, 1, 0):
            if dy or dz:
                plane.append((ys[dy], zs[dz], {"ctx": zs[dz] * 16 + ys[dy] * 2 + core}))
    rank = z * 8 + jnp.where(y < 4, y, 11 - y)
    chip_at = [t // 8 * 8 + (t % 8 if t % 8 < 4 else 11 - t % 8) for t in range(32)]

    def ranked(t):
        return {"ctx": chip_at[t] * 2 + core}

    def headed(th, tc):
        return {"ctx": chip * 2 + tc, "head": th}

    loads = [
        local(k_ref.at[:, pl.ds(mine, 256)], kv2.at[core, :, pl.ds(0, 256)], in_sem.at[0]),
        local(v_ref.at[:, pl.ds(mine, 256)], kv2.at[core, :, pl.ds(256, 256)], in_sem.at[1]),
        local(q_ref.at[:, pl.ds(mine, 256)], q2.at[core], in_sem.at[2]),
        local(gid_ref, gid, in_sem.at[3]),
        local(pat_ref, pat, in_sem.at[4]),
    ]
    for cp in loads:
        cp.start()

    bar = pltpu.get_barrier_semaphore()

    @pl.when(core == 0)
    def _():
        signal(bar, sib)

    for t in range(1, 32):

        @pl.when(t > rank)
        def _():
            signal(bar, ranked(t))

    for th in range(1, 8):

        @pl.when(th > head)
        def _():
            signal(bar, headed(th, 0))
            signal(bar, headed(th, 1))

    lower = rank + 2 * head + core

    @pl.when(lower > 0)
    def _():
        pl.semaphore_wait(bar, lower)

    @pl.when(core == 1)
    def _():
        signal(ok_sib, sib)

    for t in range(31):

        @pl.when(t < rank)
        def _():
            signal(ok_plane.at[rank], ranked(t))

    for th in range(7):

        @pl.when(th < head)
        def _():
            signal(ok_group, headed(th, 0))
            signal(ok_group, headed(th, 1))

    @pl.when(core == 0)
    def _():
        pl.semaphore_wait(ok_sib, 1)

    pairs = [
        remote(k_ref.at[:, pl.ds(theirs, 256)], kv2.at[core, :, pl.ds(0, 256)], pair_s.at[0], pair_r.at[0], sib),
        remote(v_ref.at[:, pl.ds(theirs, 256)], kv2.at[core, :, pl.ds(256, 256)], pair_s.at[1], pair_r.at[1], sib),
        remote(q_ref.at[:, pl.ds(theirs, 256)], q2.at[core], pair_s.at[2], pair_r.at[2], sib),
    ]
    for cp in pairs:
        cp.start()
    loads[0].wait()
    loads[1].wait()
    pairs[0].wait_recv()
    pairs[1].wait_recv()

    def piece(ref, tz, ty):
        return ref.at[pl.ds(pl.multiple_of(ty * 16, 16), 16), pl.ds(pl.multiple_of(tz * 128, 128), 128)]

    loads[3].wait()
    g0 = gid[0]
    cand[...] = kv2[g0 % 2]
    nbk = [
        remote(kv2.at[1], kvn.at[0], nb_s.at[0], nb_r.at[0], right),
        remote(kv2.at[0], kvn.at[1], nb_s.at[1], nb_r.at[1], left),
    ]
    right_chip = around(chip, 1, 32)
    left_chip = around(chip, 31, 32)

    def first(t):
        tz, ty = chip_at[t] // 8, chip_at[t] % 8

        @pl.when(chip == 31)
        def _():
            remote(piece(kv2.at[1], tz, ty), hold.at[1], sc_s, sc_r, ranked(t)).start()

        remote(piece(cand, tz, ty), rsel.at[chip], sel_s, sel_r, ranked(t)).start()

        @pl.when(right_chip == chip_at[t])
        def _():
            nbk[0].start()

        @pl.when(left_chip == chip_at[t])
        def _():
            nbk[1].start()

    for t in range(31):

        @pl.when(t < rank)
        def _():
            first(t)

    local(piece(cand, z, y), rsel.at[chip], sel_r).start()

    @pl.when(chip == 31)
    def _():
        local(piece(kv2.at[1], z, y), hold.at[1], sc_r).start()

    rows = pl.ds(pl.multiple_of(head * 16, 16), 16)

    def give(th, tc):
        cols = pl.ds(pl.multiple_of(th * 512 + tc * 256, 256), 256)
        return remote(g_ref.at[:, cols], do2.at[core, rows], do_s, do_r, headed(th, tc))

    give(head, 1 - core).start()
    local(g_ref.at[:, pl.ds(pl.multiple_of(head * 512 + core * 256, 256), 256)], do2.at[core, rows], do_r).start()
    for th in range(7):

        @pl.when(th < head)
        def _():
            give(th, 0).start()
            give(th, 1).start()

    for t in range(1, 32):

        @pl.when(t > rank)
        def _():
            pl.semaphore_wait(ok_plane.at[t], 1)
            first(t)

    @pl.when(head < 7)
    def _():
        pl.semaphore_wait(ok_group, 2 * (7 - head))

    for th in range(1, 8):

        @pl.when(th > head)
        def _():
            give(th, 0).start()
            give(th, 1).start()

    def spread(g):
        for _, _, dev in plane:
            remote(hold.at[g], piece(gkv.at[g], z, y), ag_s.at[g], ag_r.at[g], dev).start()

        local(hold.at[g], piece(gkv.at[g], z, y), ag_r.at[g]).start()

    wait(hold.at[1], sc_r)
    spread(1)
    wait(rsel, sel_r)
    hold[0] = rsel[g0 // 2]
    spread(0)

    loads[2].wait()
    loads[4].wait()
    pairs[2].wait_recv()
    nbk[0].wait_recv()
    nbk[1].wait_recv()
    wait(do2, do_r)

    def count(block, target):
        n = jnp.int32(1)
        for r in range(3):
            n = n + jnp.where(pat[r, block] == target, 1, 0)
        return n.astype(F32)

    b0, b1 = chip * 2, chip * 2 + 1
    bl, br = (b0 + 63) % 64, (b0 + 2) % 64
    lane = lax.broadcasted_iota(jnp.int32, (1, 256), 1) < 128
    mult = [
        jnp.where(lane, count(b0, bl), count(b1, br)),
        jnp.where(lane, count(b0, b0), count(b1, b0)),
        jnp.where(lane, count(b0, b1), count(b1, b1)),
    ]

    def cols(hh):
        return slice(hh * 128, hh * 128 + 128), slice(256 + hh * 128, 384 + hh * 128)

    stats = []
    for hh in range(2):
        kc, vc = cols(hh)
        qh = q2[:, :, kc].reshape(256, 128)
        gh = do2[:, :, kc].reshape(256, 128)
        s_out = jnp.concatenate([dot(kvn[0, :, kc], qh[:128], NT), dot(kvn[1, :, kc], qh[128:], NT)], axis=1) * SCALE
        s_in = dot(kv2[:, :, kc].reshape(256, 128), qh, NT) * SCALE
        top = jnp.maximum(jnp.max(s_out, axis=0, keepdims=True), jnp.max(s_in, axis=0, keepdims=True))
        e_out = jnp.exp(s_out - top) * mult[0]
        e_a = jnp.exp(s_in[:128] - top) * mult[1]
        e_b = jnp.exp(s_in[128:] - top) * mult[2]
        d_out = jnp.concatenate([dot(kvn[0, :, vc], gh[:128], NT), dot(kvn[1, :, vc], gh[128:], NT)], axis=1)
        d_in = dot(kv2[:, :, vc].reshape(256, 128), gh, NT)
        total = jnp.sum(e_out + e_a + e_b, axis=0, keepdims=True)
        dsum = jnp.sum(e_out * d_out + e_a * d_in[:128] + e_b * d_in[128:], axis=0, keepdims=True)
        el[hh, 0:128] = e_out
        el[hh, 128:256] = e_a
        el[hh, 256:384] = e_b
        dpl[hh, 0:128] = d_out
        dpl[hh, 128:384] = d_in
        stats.append((top, total, dsum))

    wait(gkv.at[1], ag_r.at[1])
    wait(gkv.at[0], ag_r.at[0])
    rowf = []
    for hh in range(2):
        kc, vc = cols(hh)
        top_l, total_l, dsum_l = stats[hh]
        qh = q2[:, :, kc].reshape(256, 128)
        gh = do2[:, :, kc].reshape(256, 128)
        s = dot(gkv[:, :, kc].reshape(256, 128), qh, NT) * SCALE
        dp = dot(gkv[:, :, vc].reshape(256, 128), gh, NT)
        top = jnp.maximum(top_l, jnp.max(s, axis=0, keepdims=True))
        e = jnp.exp(s - top)
        scale_l = jnp.exp(top_l - top)
        inv = 1.0 / (total_l * scale_l + jnp.sum(e, axis=0, keepdims=True))
        delta = (dsum_l * scale_l + jnp.sum(e * dp, axis=0, keepdims=True)) * inv
        p = e * inv
        ds = (p * (dp - delta) * SCALE).astype(BF)
        dsg[hh] = ds
        gpart[:, :, kc] = dot(ds, qh, NN).astype(BF).reshape(2, 128, 128)
        gpart[:, :, vc] = dot(p.astype(BF), gh, NN).astype(BF).reshape(2, 128, 128)
        rowf.append((scale_l * inv, delta))

        for dy in (4, 3, 5, 2, 6, 1, 7, 0):
            for tz in (hh, hh + 2):
                src = gpart.at[:, pl.ds(pl.multiple_of(ys[dy] * 16, 16), 16), pl.ds(tz * 128, 128)]
                dev = {"ctx": tz * 16 + ys[dy] * 2 + core}
                if dy:
                    remote(src, rgr.at[chip], rg_s, rg_r, dev).start()
                    continue

                @pl.when(z == tz)
                def _():
                    local(src, rgr.at[chip], rg_r).start()

                @pl.when(z != tz)
                def _():
                    remote(src, rgr.at[chip], rg_s, rg_r, dev).start()

    nbg = []
    for hh in range(2):
        kc, vc = cols(hh)
        qh = q2[:, :, kc].reshape(256, 128)
        gh = do2[:, :, kc].reshape(256, 128)
        rf, delta = rowf[hh]
        p0 = el[hh, 0:128] * rf
        ds0 = (p0 * (dpl[hh, 0:128] - delta) * SCALE).astype(BF)
        p0 = p0.astype(BF)
        nbo[0, hh, :, 0:128] = dot(ds0[:, :128], qh[:128], NN).astype(BF)
        nbo[0, hh, :, 128:256] = dot(p0[:, :128], gh[:128], NN).astype(BF)
        nbo[1, hh, :, 0:128] = dot(ds0[:, 128:], qh[128:], NN).astype(BF)
        nbo[1, hh, :, 128:256] = dot(p0[:, 128:], gh[128:], NN).astype(BF)
        for side, dev in ((0, left), (1, right)):
            cp = remote(nbo.at[side, hh], nbi.at[1 - side, hh], gn_s.at[side, hh], gn_r.at[1 - side, hh], dev)
            cp.start()
            nbg.append(cp)
        p1 = el[hh, 128:384] * rf
        ds1 = (p1 * (dpl[hh, 128:384] - delta) * SCALE).astype(BF)
        own[:, :, kc] = dot(ds1, qh, NN).reshape(2, 128, 128)
        own[:, :, vc] = dot(p1.astype(BF), gh, NN).reshape(2, 128, 128)
        dq = dot(ds1, kv2[:, :, kc].reshape(256, 128), TN)
        dq = dq + dot(dsg[hh], gkv[:, :, kc].reshape(256, 128), TN)
        dqb[0, :, kc] = (dq[:128] + dot(ds0[:, :128], kvn[0, :, kc], TN)).astype(BF)
        dqb[1, :, kc] = (dq[128:] + dot(ds0[:, 128:], kvn[1, :, kc], TN)).astype(BF)

    my_cols = pl.ds(mine, 256)
    outs = [
        remote(dqb.at[1 - core], all_ref.at[0, :, my_cols], out_s.at[0], out_r.at[0], sib),
        local(dqb.at[core], all_ref.at[0, :, my_cols], out_l.at[0]),
    ]
    for cp in outs:
        cp.start()

    wait(rgr, rg_r)
    acc = rgr[0].astype(F32)
    for j in range(1, 32):
        acc = acc + rgr[j].astype(F32)
    hsum[...] = acc.astype(BF)

    for _, _, dev in plane:
        remote(hsum.at[0], piece(gs0, z, y), gs_s.at[0], gs_r.at[0], dev).start()

    local(hsum.at[0], piece(gs0, z, y), gs_r.at[0]).start()

    @pl.when(chip == 31)
    def _():
        local(hsum.at[1], piece(gs63, z, y), gs_r.at[1]).start()

    @pl.when(chip != 31)
    def _():
        remote(hsum.at[1], piece(gs63, z, y), gs_s.at[1], gs_r.at[1], {"ctx": 62 + core}).start()

    for cp in nbg:
        cp.wait_recv()
    for b in range(2):
        for hh in range(2):
            kc, vc = cols(hh)
            own[b, :, kc] += nbi[b, hh, :, 0:128].astype(F32)
            own[b, :, vc] += nbi[b, hh, :, 128:256].astype(F32)

    @pl.when(chip == 31)
    def _():
        wait(gs63, gs_r.at[1])
        own[1] += gs63[...].astype(F32)

    wait(gs0, gs_r.at[0])
    for b in range(2):
        pick = jnp.where(g0 == b0 + b, 1.0, 0.0).astype(F32)
        fin[b] = (own[b] + gs0[...].astype(F32) * pick).astype(BF)

    lo, hi = pl.ds(0, 256), pl.ds(256, 256)
    more = [
        remote(fin.at[1 - core, :, lo], all_ref.at[1, :, my_cols], out_s.at[1], out_r.at[1], sib),
        remote(fin.at[1 - core, :, hi], all_ref.at[2, :, my_cols], out_s.at[2], out_r.at[2], sib),
        local(fin.at[core, :, lo], all_ref.at[1, :, my_cols], out_l.at[1]),
        local(fin.at[core, :, hi], all_ref.at[2, :, my_cols], out_l.at[2]),
    ]
    for cp in more:
        cp.start()

    for cp in pairs:
        cp.wait_send()
    for cp in nbk:
        cp.wait_send()
    for cp in nbg:
        cp.wait_send()

    @pl.when(chip == 31)
    def _():
        wait(rsel.at[pl.ds(0, 31)], sc_s)

    @pl.when(chip != 31)
    def _():
        wait(hsum.at[1], gs_s.at[1])

    wait(rsel.at[pl.ds(0, 31)], sel_s)
    wait(rsel.at[pl.ds(0, 30)], do_s)
    wait(rsel.at[pl.ds(0, 31)], ag_s.at[0])
    wait(rsel.at[pl.ds(0, 31)], ag_s.at[1])
    wait(rgr.at[pl.ds(0, 31)], rg_s)
    wait(rsel.at[pl.ds(0, 31)], gs_s.at[0])
    for cp in outs + more:
        cp.wait()


def shards(queries, key_states, values, out_grad, pattern, global_ids):
    vmem = pltpu.VMEM
    dma = pltpu.SemaphoreType.DMA
    hbm = pl.BlockSpec(memory_space=pltpu.HBM)
    anyspace = pl.BlockSpec(memory_space=pl.ANY)
    smem = pl.BlockSpec(memory_space=pltpu.SMEM)
    out = jax.ShapeDtypeStruct((3, BLK, 512), BF)
    operands = (pattern.T, global_ids, queries, key_states, values, out_grad)
    grads = pl.pallas_call(
        kernel,
        out_shape=out,
        in_specs=[hbm] * 6,
        out_specs=anyspace,
        scratch_shapes=[
            pltpu.SMEM((3, 64), jnp.int32),
            pltpu.SMEM((2,), jnp.int32),
            vmem((2, BLK, 256), BF),
            vmem((2, BLK, 512), BF),
            vmem((2, BLK, 512), BF),
            vmem((2, BLK, 256), BF),
            vmem((BLK, 512), BF),
            vmem((32, 16, 128), BF),
            vmem((2, 16, 128), BF),
            vmem((2, BLK, 512), BF),
            vmem((2, BLK, 512), BF),
            vmem((32, 2, 16, 128), BF),
            vmem((2, 16, 128), BF),
            vmem((BLK, 512), BF),
            vmem((BLK, 512), BF),
            vmem((2, 2, BLK, 256), BF),
            vmem((2, 2, BLK, 256), BF),
            vmem((2, BLK, 512), F32),
            vmem((2, BLK, 512), BF),
            vmem((2, BLK, 256), BF),
            vmem((2, 384, 256), F32),
            vmem((2, 384, 256), F32),
            vmem((2, 256, 256), BF),
            pltpu.SemaphoreType.REGULAR, pltpu.SemaphoreType.REGULAR, pltpu.SemaphoreType.REGULAR((32,)),
            dma((5,)),
            dma((3,)), dma((3,)),
            dma((2,)), dma((2,)),
            dma, dma,
            dma, dma,
            dma, dma,
            dma((2,)), dma((2,)),
            dma, dma,
            dma((2,)), dma((2,)),
            dma((2, 2)), dma((2, 2)),
            dma((3,)), dma((3,)), dma((3,)),
        ],
        name="block_attention_grads",
        compiler_params=pltpu.CompilerParams(
            collective_id=0, has_side_effects=True, vmem_limit_bytes=32 * 1024 * 1024
        ),
    )(*[pltpu.with_memory_space_constraint(a, pltpu.HBM) for a in operands])
    return grads[0], grads[1], grads[2]


def solution(mesh):
    placed = (
        P("ctx", "head"),
        P("ctx", "head"),
        P("ctx", "head"),
        P(("ctx", "head"), None),
        P(),
        P(),
    )
    return jax.shard_map(
        shards,
        mesh=mesh,
        in_specs=placed,
        out_specs=(P("ctx", "head"), P("ctx", "head"), P("ctx", "head")),
        check_vma=False,
    )
```

```python
import functools
import math

import jax
import jax.numpy as jnp
from jax import lax
from jax.experimental import pallas as pl
from jax.experimental.pallas import tpu as pltpu
from jax.sharding import PartitionSpec as P

HD = 128
BLK = 128
SCALE = 1.0 / math.sqrt(HD)
MESH = pl.DeviceIdType.MESH
BF = jnp.bfloat16
F32 = jnp.float32
NT = (((1,), (1,)), ((), ()))
NN = (((1,), (0,)), ((), ()))
TN = (((0,), (0,)), ((), ()))


def remote(src, dst, ss, rs, dev):
    return pltpu.make_async_remote_copy(
        src_ref=src, dst_ref=dst, send_sem=ss, recv_sem=rs,
        device_id=dev, device_id_type=MESH,
    )


def local(src, dst, sem):
    return pltpu.make_async_copy(src, dst, sem)


def wait(ref, sem):
    pltpu.make_async_copy(ref, ref, sem).wait()


def signal(sem, dev):
    pl.semaphore_signal(sem, inc=1, device_id=dev, device_id_type=MESH)


def dot(a, b, dims):
    return lax.dot_general(a, b, dims, preferred_element_type=F32)


def kernel(
    pat_ref, gid_ref, q_ref, k_ref, v_ref, g_ref, all_ref,
    pat, gid, q2, kv2, kvn, do2, cand, rsel, hold, gkv, gpart, rgr, hsum, gs0, gs63,
    nbo, nbi, own, fin, dqb, el, dpl, dsg,
    ok_sib, ok_group, ok_plane, in_sem, pair_s, pair_r, nb_s, nb_r, do_s, do_r, sel_s, sel_r, sc_s, sc_r,
    ag_s, ag_r, rg_s, rg_r, gs_s, gs_r, gn_s, gn_r, out_l, out_s, out_r,
):
    me = lax.axis_index("ctx")
    head = lax.axis_index("head")
    core = me % 2
    chip = me // 2
    y = chip % 8
    z = chip // 8
    sib = {"ctx": chip * 2 + 1 - core}
    left = {"ctx": (me + 62) % 64}
    right = {"ctx": (me + 2) % 64}
    mine = pl.multiple_of(core * 256, 256)
    theirs = pl.multiple_of((1 - core) * 256, 256)

    def around(base, step, size):
        return jnp.where(base + step >= size, base + step - size, base + step)

    ys = [around(y, d, 8) for d in range(8)]
    zs = [around(z, d, 4) for d in range(4)]
    plane = []
    for dy in (4, 3, 5, 2, 6, 1, 7, 0):
        for dz in (3, 2, 1, 0):
            if dy or dz:
                plane.append((ys[dy], zs[dz], {"ctx": zs[dz] * 16 + ys[dy] * 2 + core}))
    row = z * 8
    above = row + 8

    def at_chip(t):
        return {"ctx": t * 2 + core}

    def headed(th, tc):
        return {"ctx": chip * 2 + tc, "head": th}

    loads = [
        local(k_ref.at[:, pl.ds(mine, 256)], kv2.at[core, :, pl.ds(0, 256)], in_sem.at[0]),
        local(v_ref.at[:, pl.ds(mine, 256)], kv2.at[core, :, pl.ds(256, 256)], in_sem.at[1]),
        local(q_ref.at[:, pl.ds(mine, 256)], q2.at[core], in_sem.at[2]),
        local(gid_ref, gid, in_sem.at[3]),
        local(pat_ref, pat, in_sem.at[4]),
    ]
    for cp in loads:
        cp.start()

    bar = pltpu.get_barrier_semaphore()

    @pl.when(core == 0)
    def _():
        signal(bar, sib)

    @pl.loop(row, chip)
    def _(t):
        signal(bar, at_chip(t))

    @pl.loop(chip + 1, 32)
    def _(t):
        signal(bar, at_chip(t))

    @pl.loop(head + 1, 8)
    def _(th):
        signal(bar, headed(th, 0))
        signal(bar, headed(th, 1))

    pl.semaphore_wait(bar, row + 7 + 2 * head + core)

    @pl.when(core == 1)
    def _():
        signal(ok_sib, sib)

    @pl.loop(0, row)
    def _(t):
        signal(ok_plane.at[chip], at_chip(t))

    @pl.loop(0, head)
    def _(th):
        signal(ok_group, headed(th, 0))
        signal(ok_group, headed(th, 1))

    @pl.when(core == 0)
    def _():
        pl.semaphore_wait(ok_sib, 1)

    pairs = [
        remote(k_ref.at[:, pl.ds(theirs, 256)], kv2.at[core, :, pl.ds(0, 256)], pair_s.at[0], pair_r.at[0], sib),
        remote(v_ref.at[:, pl.ds(theirs, 256)], kv2.at[core, :, pl.ds(256, 256)], pair_s.at[1], pair_r.at[1], sib),
        remote(q_ref.at[:, pl.ds(theirs, 256)], q2.at[core], pair_s.at[2], pair_r.at[2], sib),
    ]
    for cp in pairs:
        cp.start()
    loads[0].wait()
    loads[1].wait()
    pairs[0].wait_recv()
    pairs[1].wait_recv()

    def piece(ref, tz, ty):
        return ref.at[pl.ds(pl.multiple_of(ty * 16, 16), 16), pl.ds(pl.multiple_of(tz * 128, 128), 128)]

    loads[3].wait()
    g0 = gid[0]
    cand[...] = kv2[g0 % 2]
    nbk = [
        remote(kv2.at[1], kvn.at[0], nb_s.at[0], nb_r.at[0], right),
        remote(kv2.at[0], kvn.at[1], nb_s.at[1], nb_r.at[1], left),
    ]
    right_chip = around(chip, 1, 32)
    left_chip = around(chip, 31, 32)

    def first(t):
        remote(piece(cand, t // 8, t % 8), rsel.at[chip], sel_s, sel_r, at_chip(t)).start()

    def root(t):
        remote(piece(kv2.at[1], t // 8, t % 8), hold.at[1], sc_s, sc_r, at_chip(t)).start()

    pl.loop(0, chip)(first)
    pl.loop(chip + 1, above)(first)

    @pl.when(chip == 31)
    def _():
        pl.loop(0, 31)(root)
        local(piece(kv2.at[1], z, y), hold.at[1], sc_r).start()

    local(piece(cand, z, y), rsel.at[chip], sel_r).start()

    rows = pl.ds(pl.multiple_of(head * 16, 16), 16)

    def give(th, tc):
        cols = pl.ds(pl.multiple_of(th * 512 + tc * 256, 256), 256)
        return remote(g_ref.at[:, cols], do2.at[core, rows], do_s, do_r, headed(th, tc))

    give(head, 1 - core).start()
    local(g_ref.at[:, pl.ds(pl.multiple_of(head * 512 + core * 256, 256), 256)], do2.at[core, rows], do_r).start()

    @pl.loop(0, head)
    def _(th):
        give(th, 0).start()
        give(th, 1).start()

    def rest(t):
        pl.semaphore_wait(ok_plane.at[t], 1)
        first(t)

    split = jnp.maximum(above, 24)
    pl.loop(above, split)(rest)
    pl.loop(split, 32)(rest)
    for cp in nbk:
        cp.start()


    def spread(g):
        for _, _, dev in plane:
            remote(hold.at[g], piece(gkv.at[g], z, y), ag_s.at[g], ag_r.at[g], dev).start()

        local(hold.at[g], piece(gkv.at[g], z, y), ag_r.at[g]).start()

    wait(hold.at[1], sc_r)
    spread(1)
    wait(rsel, sel_r)
    hold[0] = rsel[g0 // 2]
    spread(0)

    @pl.when(head < 7)
    def _():
        pl.semaphore_wait(ok_group, 2 * (7 - head))

    @pl.loop(head + 1, 8)
    def _(th):
        give(th, 0).start()
        give(th, 1).start()

    loads[2].wait()
    loads[4].wait()
    pairs[2].wait_recv()
    nbk[0].wait_recv()
    nbk[1].wait_recv()
    wait(do2, do_r)

    def count(block, target):
        n = jnp.int32(1)
        for r in range(3):
            n = n + jnp.where(pat[r, block] == target, 1, 0)
        return n.astype(F32)

    b0, b1 = chip * 2, chip * 2 + 1
    bl, br = (b0 + 63) % 64, (b0 + 2) % 64
    lane = lax.broadcasted_iota(jnp.int32, (1, 256), 1) < 128
    mult = [
        jnp.where(lane, count(b0, bl), count(b1, br)),
        jnp.where(lane, count(b0, b0), count(b1, b0)),
        jnp.where(lane, count(b0, b1), count(b1, b1)),
    ]

    def cols(hh):
        return slice(hh * 128, hh * 128 + 128), slice(256 + hh * 128, 384 + hh * 128)

    stats = []
    for hh in range(2):
        kc, vc = cols(hh)
        qh = q2[:, :, kc].reshape(256, 128)
        gh = do2[:, :, kc].reshape(256, 128)
        s_out = jnp.concatenate([dot(kvn[0, :, kc], qh[:128], NT), dot(kvn[1, :, kc], qh[128:], NT)], axis=1) * SCALE
        s_in = dot(kv2[:, :, kc].reshape(256, 128), qh, NT) * SCALE
        top = jnp.maximum(jnp.max(s_out, axis=0, keepdims=True), jnp.max(s_in, axis=0, keepdims=True))
        e_out = jnp.exp(s_out - top) * mult[0]
        e_a = jnp.exp(s_in[:128] - top) * mult[1]
        e_b = jnp.exp(s_in[128:] - top) * mult[2]
        d_out = jnp.concatenate([dot(kvn[0, :, vc], gh[:128], NT), dot(kvn[1, :, vc], gh[128:], NT)], axis=1)
        d_in = dot(kv2[:, :, vc].reshape(256, 128), gh, NT)
        total = jnp.sum(e_out + e_a + e_b, axis=0, keepdims=True)
        dsum = jnp.sum(e_out * d_out + e_a * d_in[:128] + e_b * d_in[128:], axis=0, keepdims=True)
        el[hh, 0:128] = e_out
        el[hh, 128:256] = e_a
        el[hh, 256:384] = e_b
        dpl[hh, 0:128] = d_out
        dpl[hh, 128:384] = d_in
        stats.append((top, total, dsum))

    wait(gkv.at[1], ag_r.at[1])
    wait(gkv.at[0], ag_r.at[0])
    rowf = []

    def reduce_to(g, tz, dy):
        src = gpart.at[g, pl.ds(pl.multiple_of(ys[dy] * 16, 16), 16), pl.ds(tz * 128, 128)]
        dst = rgr.at[g, chip]
        push = remote(src, dst, rg_s.at[g], rg_r.at[g], {"ctx": tz * 16 + ys[dy] * 2 + core})
        if dy:
            push.start()
            return

        @pl.when(z == tz)
        def _():
            local(src, dst, rg_r.at[g]).start()

        @pl.when(z != tz)
        def _():
            push.start()

    for hh in range(2):
        kc, vc = cols(hh)
        top_l, total_l, dsum_l = stats[hh]
        qh = q2[:, :, kc].reshape(256, 128)
        gh = do2[:, :, kc].reshape(256, 128)
        s = dot(gkv[:, :, kc].reshape(256, 128), qh, NT) * SCALE
        dp = dot(gkv[:, :, vc].reshape(256, 128), gh, NT)
        top = jnp.maximum(top_l, jnp.max(s, axis=0, keepdims=True))
        e = jnp.exp(s - top)
        scale_l = jnp.exp(top_l - top)
        inv = 1.0 / (total_l * scale_l + jnp.sum(e, axis=0, keepdims=True))
        delta = (dsum_l * scale_l + jnp.sum(e * dp, axis=0, keepdims=True)) * inv
        p = e * inv
        ds = (p * (dp - delta) * SCALE).astype(BF)
        dsg[hh] = ds
        gpart[:, :, kc] = dot(ds, qh, NN).astype(BF).reshape(2, 128, 128)
        gpart[:, :, vc] = dot(p.astype(BF), gh, NN).astype(BF).reshape(2, 128, 128)
        rowf.append((scale_l * inv, delta))

        for dy in (4, 3, 5, 2, 6, 1, 7, 0):
            for tz in (hh, hh + 2):
                reduce_to(0, tz, dy)

    for dy in (4, 3, 5, 2, 6, 1, 7, 0):
        for tz in range(4):
            reduce_to(1, tz, dy)

    nbg = []
    for hh in range(2):
        kc, vc = cols(hh)
        qh = q2[:, :, kc].reshape(256, 128)
        gh = do2[:, :, kc].reshape(256, 128)
        rf, delta = rowf[hh]
        p0 = el[hh, 0:128] * rf
        ds0 = (p0 * (dpl[hh, 0:128] - delta) * SCALE).astype(BF)
        p0 = p0.astype(BF)
        nbo[0, hh, :, 0:128] = dot(ds0[:, :128], qh[:128], NN).astype(BF)
        nbo[0, hh, :, 128:256] = dot(p0[:, :128], gh[:128], NN).astype(BF)
        nbo[1, hh, :, 0:128] = dot(ds0[:, 128:], qh[128:], NN).astype(BF)
        nbo[1, hh, :, 128:256] = dot(p0[:, 128:], gh[128:], NN).astype(BF)
        for side, dev in ((0, left), (1, right)):
            nbg.append(remote(nbo.at[side, hh], nbi.at[1 - side, hh], gn_s.at[side, hh], gn_r.at[1 - side, hh], dev))

        @pl.when(chip == 31)
        def _():
            nbg[-1].start()

        p1 = el[hh, 128:384] * rf
        ds1 = (p1 * (dpl[hh, 128:384] - delta) * SCALE).astype(BF)
        own[:, :, kc] = dot(ds1, qh, NN).reshape(2, 128, 128)
        own[:, :, vc] = dot(p1.astype(BF), gh, NN).reshape(2, 128, 128)
        dq = dot(ds1, kv2[:, :, kc].reshape(256, 128), TN)
        dq = dq + dot(dsg[hh], gkv[:, :, kc].reshape(256, 128), TN)
        dqb[0, :, kc] = (dq[:128] + dot(ds0[:, :128], kvn[0, :, kc], TN)).astype(BF)
        dqb[1, :, kc] = (dq[128:] + dot(ds0[:, 128:], kvn[1, :, kc], TN)).astype(BF)

    my_cols = pl.ds(mine, 256)
    outs = [
        remote(dqb.at[1 - core], all_ref.at[0, :, my_cols], out_s.at[0], out_r.at[0], sib),
        local(dqb.at[core], all_ref.at[0, :, my_cols], out_l.at[0]),
    ]
    for cp in outs:
        cp.start()

    def total(g):
        wait(rgr.at[g], rg_r.at[g])
        acc = rgr[g, 0].astype(F32)
        for j in range(1, 32):
            acc = acc + rgr[g, j].astype(F32)
        hsum[g] = acc.astype(BF)

    total(0)
    for tz in range(4):
        for dy in (4, 3, 5, 2, 6, 1, 7):
            dev = {"ctx": tz * 16 + ys[dy] * 2 + core}
            remote(hsum.at[0], piece(gs0, z, y), gs_s.at[0], gs_r.at[0], dev).start()

        @pl.when(z != tz)
        def _():
            dev = {"ctx": tz * 16 + y * 2 + core}
            remote(hsum.at[0], piece(gs0, z, y), gs_s.at[0], gs_r.at[0], dev).start()

    local(hsum.at[0], piece(gs0, z, y), gs_r.at[0]).start()
    nbg[0].start()
    nbg[2].start()

    @pl.when(chip != 31)
    def _():
        nbg[1].start()
        nbg[3].start()

    for cp in nbg:
        cp.wait_recv()
    for b in range(2):
        for hh in range(2):
            kc, vc = cols(hh)
            own[b, :, kc] += nbi[b, hh, :, 0:128].astype(F32)
            own[b, :, vc] += nbi[b, hh, :, 128:256].astype(F32)
    wait(gs0, gs_r.at[0])
    lo, hi = pl.ds(0, 256), pl.ds(256, 256)
    more = [
        remote(fin.at[1 - core, :, lo], all_ref.at[1, :, my_cols], out_s.at[1], out_r.at[1], sib),
        remote(fin.at[1 - core, :, hi], all_ref.at[2, :, my_cols], out_s.at[2], out_r.at[2], sib),
        local(fin.at[core, :, lo], all_ref.at[1, :, my_cols], out_l.at[1]),
        local(fin.at[core, :, hi], all_ref.at[2, :, my_cols], out_l.at[2]),
    ]

    def finish():
        for b in range(2):
            pick = jnp.where(g0 == b0 + b, 1.0, 0.0).astype(F32)
            fin[b] = (own[b] + gs0[...].astype(F32) * pick).astype(BF)
        for cp in more:
            cp.start()

    @pl.when(chip != 31)
    def _():
        finish()

    total(1)

    @pl.when(chip == 31)
    def _():
        local(hsum.at[1], piece(gs63, z, y), gs_r.at[1]).start()
        wait(gs63, gs_r.at[1])
        own[1] += gs63[...].astype(F32)
        finish()

    @pl.when(chip != 31)
    def _():
        remote(hsum.at[1], piece(gs63, z, y), gs_s.at[1], gs_r.at[1], {"ctx": 62 + core}).start()

    for cp in pairs:
        cp.wait_send()
    for cp in nbk:
        cp.wait_send()
    for cp in nbg:
        cp.wait_send()

    @pl.when(chip == 31)
    def _():
        wait(rsel.at[pl.ds(0, 31)], sc_s)

    @pl.when(chip != 31)
    def _():
        wait(hsum.at[1], gs_s.at[1])

    wait(rsel.at[pl.ds(0, 31)], sel_s)
    wait(rsel.at[pl.ds(0, 30)], do_s)
    wait(rsel.at[pl.ds(0, 31)], ag_s.at[0])
    wait(rsel.at[pl.ds(0, 31)], ag_s.at[1])
    wait(rsel.at[pl.ds(0, 31)], rg_s.at[0])
    wait(rsel.at[pl.ds(0, 31)], rg_s.at[1])
    wait(rsel.at[pl.ds(0, 31)], gs_s.at[0])
    for cp in outs + more:
        cp.wait()


def shards(queries, key_states, values, out_grad, pattern, global_ids):
    vmem = pltpu.VMEM
    dma = pltpu.SemaphoreType.DMA
    hbm = pl.BlockSpec(memory_space=pltpu.HBM)
    anyspace = pl.BlockSpec(memory_space=pl.ANY)
    smem = pl.BlockSpec(memory_space=pltpu.SMEM)
    out = jax.ShapeDtypeStruct((3, BLK, 512), BF)
    operands = (pattern.T, global_ids, queries, key_states, values, out_grad)
    grads = pl.pallas_call(
        kernel,
        out_shape=out,
        in_specs=[hbm] * 6,
        out_specs=anyspace,
        scratch_shapes=[
            pltpu.SMEM((3, 64), jnp.int32),
            pltpu.SMEM((2,), jnp.int32),
            vmem((2, BLK, 256), BF),
            vmem((2, BLK, 512), BF),
            vmem((2, BLK, 512), BF),
            vmem((2, BLK, 256), BF),
            vmem((BLK, 512), BF),
            vmem((32, 16, 128), BF),
            vmem((2, 16, 128), BF),
            vmem((2, BLK, 512), BF),
            vmem((2, BLK, 512), BF),
            vmem((2, 32, 16, 128), BF),
            vmem((2, 16, 128), BF),
            vmem((BLK, 512), BF),
            vmem((BLK, 512), BF),
            vmem((2, 2, BLK, 256), BF),
            vmem((2, 2, BLK, 256), BF),
            vmem((2, BLK, 512), F32),
            vmem((2, BLK, 512), BF),
            vmem((2, BLK, 256), BF),
            vmem((2, 384, 256), F32),
            vmem((2, 384, 256), F32),
            vmem((2, 256, 256), BF),
            pltpu.SemaphoreType.REGULAR, pltpu.SemaphoreType.REGULAR, pltpu.SemaphoreType.REGULAR((32,)),
            dma((5,)),
            dma((3,)), dma((3,)),
            dma((2,)), dma((2,)),
            dma, dma,
            dma, dma,
            dma, dma,
            dma((2,)), dma((2,)),
            dma((2,)), dma((2,)),
            dma((2,)), dma((2,)),
            dma((2, 2)), dma((2, 2)),
            dma((3,)), dma((3,)), dma((3,)),
        ],
        name="block_attention_grads",
        compiler_params=pltpu.CompilerParams(
            collective_id=0, has_side_effects=True, vmem_limit_bytes=32 * 1024 * 1024
        ),
    )(*[pltpu.with_memory_space_constraint(a, pltpu.HBM) for a in operands])
    return grads[0], grads[1], grads[2]


def solution(mesh):
    placed = (
        P("ctx", "head"),
        P("ctx", "head"),
        P("ctx", "head"),
        P(("ctx", "head"), None),
        P(),
        P(),
    )
    return jax.shard_map(
        shards,
        mesh=mesh,
        in_specs=placed,
        out_specs=(P("ctx", "head"), P("ctx", "head"), P("ctx", "head")),
        check_vma=False,
    )
```

```python
import functools
import math

import jax
import jax.numpy as jnp
from jax import lax
from jax.experimental import pallas as pl
from jax.experimental.pallas import tpu as pltpu
from jax.sharding import PartitionSpec as P

HD = 128
BLK = 128
SCALE = 1.0 / math.sqrt(HD)
MESH = pl.DeviceIdType.MESH
BF = jnp.bfloat16
F32 = jnp.float32
NT = (((1,), (1,)), ((), ()))
NN = (((1,), (0,)), ((), ()))
TN = (((0,), (0,)), ((), ()))


def remote(src, dst, ss, rs, dev):
    return pltpu.make_async_remote_copy(
        src_ref=src, dst_ref=dst, send_sem=ss, recv_sem=rs,
        device_id=dev, device_id_type=MESH,
    )


def local(src, dst, sem):
    return pltpu.make_async_copy(src, dst, sem)


def wait(ref, sem):
    pltpu.make_async_copy(ref, ref, sem).wait()


def signal(sem, dev):
    pl.semaphore_signal(sem, inc=1, device_id=dev, device_id_type=MESH)


def dot(a, b, dims):
    return lax.dot_general(a, b, dims, preferred_element_type=F32)


def kernel(
    pat_ref, gid_ref, q_ref, k_ref, v_ref, g_ref, all_ref,
    pat, gid, q2, kv2, kvn, do2, cand, rsel, hold, gkv, gpart, rgr, hsum, gs0, gs63,
    nbo, nbi, own, fin, dqb, el, dpl, dsg,
    ok_sib, ok_group, ok_plane, in_sem, pair_s, pair_r, nb_s, nb_r, do_s, do_r, sel_s, sel_r, sc_s, sc_r,
    ag_s, ag_r, rg_s, rg_r, gs_s, gs_r, gn_s, gn_r, out_l, out_s, out_r,
):
    me = lax.axis_index("ctx")
    head = lax.axis_index("head")
    core = me % 2
    chip = me // 2
    y = chip % 8
    z = chip // 8
    sib = {"ctx": chip * 2 + 1 - core}
    left = {"ctx": (me + 62) % 64}
    right = {"ctx": (me + 2) % 64}
    mine = pl.multiple_of(core * 256, 256)
    theirs = pl.multiple_of((1 - core) * 256, 256)

    def around(base, step, size):
        return jnp.where(base + step >= size, base + step - size, base + step)

    ys = [around(y, d, 8) for d in range(8)]
    zs = [around(z, d, 4) for d in range(4)]
    plane = []
    for dy in (4, 3, 5, 2, 6, 1, 7, 0):
        for dz in (3, 2, 1, 0):
            if dy or dz:
                plane.append((ys[dy], zs[dz], {"ctx": zs[dz] * 16 + ys[dy] * 2 + core}))
    row = z * 8
    above = row + 8

    def at_chip(t):
        return {"ctx": t * 2 + core}

    def headed(th, tc):
        return {"ctx": chip * 2 + tc, "head": th}

    bar = pltpu.get_barrier_semaphore()

    @pl.when(core == 0)
    def _():
        signal(bar, sib)

    @pl.loop(row, chip)
    def _(t):
        signal(bar, at_chip(t))

    @pl.loop(chip + 1, 32)
    def _(t):
        signal(bar, at_chip(t))

    @pl.loop(head + 1, 8)
    def _(th):
        signal(bar, headed(th, 0))
        signal(bar, headed(th, 1))

    loads = [
        local(k_ref.at[:, pl.ds(mine, 256)], kv2.at[core, :, pl.ds(0, 256)], in_sem.at[0]),
        local(v_ref.at[:, pl.ds(mine, 256)], kv2.at[core, :, pl.ds(256, 256)], in_sem.at[1]),
        local(q_ref.at[:, pl.ds(mine, 256)], q2.at[core], in_sem.at[2]),
        local(gid_ref, gid, in_sem.at[3]),
        local(pat_ref, pat, in_sem.at[4]),
    ]
    for cp in loads:
        cp.start()

    pl.semaphore_wait(bar, row + 7 + 2 * head + core)

    @pl.when(core == 1)
    def _():
        signal(ok_sib, sib)

    @pl.loop(0, row)
    def _(t):
        signal(ok_plane.at[chip], at_chip(t))

    @pl.loop(0, head)
    def _(th):
        signal(ok_group, headed(th, 0))
        signal(ok_group, headed(th, 1))

    @pl.when(core == 0)
    def _():
        pl.semaphore_wait(ok_sib, 1)

    pairs = [
        remote(k_ref.at[:, pl.ds(theirs, 256)], kv2.at[core, :, pl.ds(0, 256)], pair_s.at[0], pair_r.at[0], sib),
        remote(v_ref.at[:, pl.ds(theirs, 256)], kv2.at[core, :, pl.ds(256, 256)], pair_s.at[1], pair_r.at[1], sib),
        remote(q_ref.at[:, pl.ds(theirs, 256)], q2.at[core], pair_s.at[2], pair_r.at[2], sib),
    ]
    for cp in pairs:
        cp.start()
    loads[0].wait()
    loads[1].wait()
    pairs[0].wait_recv()
    pairs[1].wait_recv()

    def piece(ref, tz, ty):
        return ref.at[pl.ds(pl.multiple_of(ty * 16, 16), 16), pl.ds(pl.multiple_of(tz * 128, 128), 128)]

    loads[3].wait()
    g0 = gid[0]
    cand[...] = kv2[g0 % 2]
    nbk = [
        remote(kv2.at[1], kvn.at[0], nb_s.at[0], nb_r.at[0], right),
        remote(kv2.at[0], kvn.at[1], nb_s.at[1], nb_r.at[1], left),
    ]
    right_chip = around(chip, 1, 32)
    left_chip = around(chip, 31, 32)

    def first(t):
        remote(piece(cand, t // 8, t % 8), rsel.at[chip], sel_s, sel_r, at_chip(t)).start()

    def root(t):
        remote(piece(kv2.at[1], t // 8, t % 8), hold.at[1], sc_s, sc_r, at_chip(t)).start()

    pl.loop(0, chip)(first)
    pl.loop(chip + 1, above)(first)

    @pl.when(chip == 31)
    def _():
        pl.loop(0, 31)(root)
        local(piece(kv2.at[1], z, y), hold.at[1], sc_r).start()

    local(piece(cand, z, y), rsel.at[chip], sel_r).start()

    rows = pl.ds(pl.multiple_of(head * 16, 16), 16)

    def give(th, tc):
        cols = pl.ds(pl.multiple_of(th * 512 + tc * 256, 256), 256)
        return remote(g_ref.at[:, cols], do2.at[core, rows], do_s, do_r, headed(th, tc))

    give(head, 1 - core).start()
    local(g_ref.at[:, pl.ds(pl.multiple_of(head * 512 + core * 256, 256), 256)], do2.at[core, rows], do_r).start()

    @pl.loop(0, head)
    def _(th):
        give(th, 0).start()
        give(th, 1).start()

    def rest(t):
        pl.semaphore_wait(ok_plane.at[t], 1)
        first(t)

    split = jnp.maximum(above, 24)
    pl.loop(above, split)(rest)
    pl.loop(split, 32)(rest)
    for cp in nbk:
        cp.start()


    def spread(g):
        for _, _, dev in plane:
            remote(hold.at[g], piece(gkv.at[g], z, y), ag_s.at[g], ag_r.at[g], dev).start()

        local(hold.at[g], piece(gkv.at[g], z, y), ag_r.at[g]).start()

    wait(hold.at[1], sc_r)
    spread(1)
    wait(rsel, sel_r)
    hold[0] = rsel[g0 // 2]
    spread(0)

    @pl.when(head < 7)
    def _():
        pl.semaphore_wait(ok_group, 2 * (7 - head))

    @pl.loop(head + 1, 8)
    def _(th):
        give(th, 0).start()
        give(th, 1).start()

    loads[2].wait()
    loads[4].wait()
    pairs[2].wait_recv()
    nbk[0].wait_recv()
    nbk[1].wait_recv()
    wait(do2, do_r)

    def count(block, target):
        n = jnp.int32(1)
        for r in range(3):
            n = n + jnp.where(pat[r, block] == target, 1, 0)
        return n.astype(F32)

    b0, b1 = chip * 2, chip * 2 + 1
    bl, br = (b0 + 63) % 64, (b0 + 2) % 64
    lane = lax.broadcasted_iota(jnp.int32, (1, 256), 1) < 128
    mult = [
        jnp.where(lane, count(b0, bl), count(b1, br)),
        jnp.where(lane, count(b0, b0), count(b1, b0)),
        jnp.where(lane, count(b0, b1), count(b1, b1)),
    ]

    def cols(hh):
        return slice(hh * 128, hh * 128 + 128), slice(256 + hh * 128, 384 + hh * 128)

    stats = []
    for hh in range(2):
        kc, vc = cols(hh)
        qh = q2[:, :, kc].reshape(256, 128)
        gh = do2[:, :, kc].reshape(256, 128)
        s_out = jnp.concatenate([dot(kvn[0, :, kc], qh[:128], NT), dot(kvn[1, :, kc], qh[128:], NT)], axis=1) * SCALE
        s_in = dot(kv2[:, :, kc].reshape(256, 128), qh, NT) * SCALE
        top = jnp.maximum(jnp.max(s_out, axis=0, keepdims=True), jnp.max(s_in, axis=0, keepdims=True))
        e_out = jnp.exp(s_out - top) * mult[0]
        e_a = jnp.exp(s_in[:128] - top) * mult[1]
        e_b = jnp.exp(s_in[128:] - top) * mult[2]
        d_out = jnp.concatenate([dot(kvn[0, :, vc], gh[:128], NT), dot(kvn[1, :, vc], gh[128:], NT)], axis=1)
        d_in = dot(kv2[:, :, vc].reshape(256, 128), gh, NT)
        total = jnp.sum(e_out + e_a + e_b, axis=0, keepdims=True)
        dsum = jnp.sum(e_out * d_out + e_a * d_in[:128] + e_b * d_in[128:], axis=0, keepdims=True)
        el[hh, 0:128] = e_out
        el[hh, 128:256] = e_a
        el[hh, 256:384] = e_b
        dpl[hh, 0:128] = d_out
        dpl[hh, 128:384] = d_in
        stats.append((top, total, dsum))

    wait(gkv.at[1], ag_r.at[1])
    wait(gkv.at[0], ag_r.at[0])
    rowf = []

    def reduce_to(g, tz, dy):
        src = gpart.at[g, pl.ds(pl.multiple_of(ys[dy] * 16, 16), 16), pl.ds(tz * 128, 128)]
        dst = rgr.at[g, chip]
        push = remote(src, dst, rg_s.at[g], rg_r.at[g], {"ctx": tz * 16 + ys[dy] * 2 + core})
        if dy:
            push.start()
            return

        @pl.when(z == tz)
        def _():
            local(src, dst, rg_r.at[g]).start()

        @pl.when(z != tz)
        def _():
            push.start()

    for hh in range(2):
        kc, vc = cols(hh)
        top_l, total_l, dsum_l = stats[hh]
        qh = q2[:, :, kc].reshape(256, 128)
        gh = do2[:, :, kc].reshape(256, 128)
        s = dot(gkv[:, :, kc].reshape(256, 128), qh, NT) * SCALE
        dp = dot(gkv[:, :, vc].reshape(256, 128), gh, NT)
        top = jnp.maximum(top_l, jnp.max(s, axis=0, keepdims=True))
        e = jnp.exp(s - top)
        scale_l = jnp.exp(top_l - top)
        inv = 1.0 / (total_l * scale_l + jnp.sum(e, axis=0, keepdims=True))
        delta = (dsum_l * scale_l + jnp.sum(e * dp, axis=0, keepdims=True)) * inv
        p = e * inv
        ds = (p * (dp - delta) * SCALE).astype(BF)
        dsg[hh] = ds
        gpart[:, :, kc] = dot(ds, qh, NN).astype(BF).reshape(2, 128, 128)
        gpart[:, :, vc] = dot(p.astype(BF), gh, NN).astype(BF).reshape(2, 128, 128)
        rowf.append((scale_l * inv, delta))

        for dy in (4, 3, 5, 2, 6, 1, 7, 0):
            for tz in (hh, hh + 2):
                reduce_to(0, tz, dy)

    for dy in (4, 3, 5, 2, 6, 1, 7, 0):
        for tz in range(4):
            reduce_to(1, tz, dy)

    nbg = []
    for hh in range(2):
        kc, vc = cols(hh)
        qh = q2[:, :, kc].reshape(256, 128)
        gh = do2[:, :, kc].reshape(256, 128)
        rf, delta = rowf[hh]
        p0 = el[hh, 0:128] * rf
        ds0 = (p0 * (dpl[hh, 0:128] - delta) * SCALE).astype(BF)
        p0 = p0.astype(BF)
        nbo[0, hh, :, 0:128] = dot(ds0[:, :128], qh[:128], NN).astype(BF)
        nbo[0, hh, :, 128:256] = dot(p0[:, :128], gh[:128], NN).astype(BF)
        nbo[1, hh, :, 0:128] = dot(ds0[:, 128:], qh[128:], NN).astype(BF)
        nbo[1, hh, :, 128:256] = dot(p0[:, 128:], gh[128:], NN).astype(BF)
        for side, dev in ((0, left), (1, right)):
            nbg.append(remote(nbo.at[side, hh], nbi.at[1 - side, hh], gn_s.at[side, hh], gn_r.at[1 - side, hh], dev))

        @pl.when(chip == 31)
        def _():
            nbg[-1].start()

        p1 = el[hh, 128:384] * rf
        ds1 = (p1 * (dpl[hh, 128:384] - delta) * SCALE).astype(BF)
        own[:, :, kc] = dot(ds1, qh, NN).reshape(2, 128, 128)
        own[:, :, vc] = dot(p1.astype(BF), gh, NN).reshape(2, 128, 128)
        dq = dot(ds1, kv2[:, :, kc].reshape(256, 128), TN)
        dq = dq + dot(dsg[hh], gkv[:, :, kc].reshape(256, 128), TN)
        dqb[0, :, kc] = (dq[:128] + dot(ds0[:, :128], kvn[0, :, kc], TN)).astype(BF)
        dqb[1, :, kc] = (dq[128:] + dot(ds0[:, 128:], kvn[1, :, kc], TN)).astype(BF)

    my_cols = pl.ds(mine, 256)
    outs = [
        remote(dqb.at[1 - core], all_ref.at[0, :, my_cols], out_s.at[0], out_r.at[0], sib),
        local(dqb.at[core], all_ref.at[0, :, my_cols], out_l.at[0]),
    ]
    def total(g):
        wait(rgr.at[g], rg_r.at[g])
        acc = rgr[g, 0].astype(F32)
        for j in range(1, 32):
            acc = acc + rgr[g, j].astype(F32)
        hsum[g] = acc.astype(BF)

    total(0)
    for tz in range(4):
        for dy in (4, 3, 5, 2, 6, 1, 7):
            dev = {"ctx": tz * 16 + ys[dy] * 2 + core}
            remote(hsum.at[0], piece(gs0, z, y), gs_s.at[0], gs_r.at[0], dev).start()

        @pl.when(z != tz)
        def _():
            dev = {"ctx": tz * 16 + y * 2 + core}
            remote(hsum.at[0], piece(gs0, z, y), gs_s.at[0], gs_r.at[0], dev).start()

    local(hsum.at[0], piece(gs0, z, y), gs_r.at[0]).start()
    for cp in outs:
        cp.start()
    nbg[0].start()
    nbg[2].start()

    @pl.when(chip != 31)
    def _():
        nbg[1].start()
        nbg[3].start()

    for cp in nbg:
        cp.wait_recv()
    for b in range(2):
        for hh in range(2):
            kc, vc = cols(hh)
            own[b, :, kc] += nbi[b, hh, :, 0:128].astype(F32)
            own[b, :, vc] += nbi[b, hh, :, 128:256].astype(F32)
    total(1)

    @pl.when(chip != 31)
    def _():
        remote(hsum.at[1], piece(gs63, z, y), gs_s.at[1], gs_r.at[1], {"ctx": 62 + core}).start()

    wait(gs0, gs_r.at[0])
    lo, hi = pl.ds(0, 256), pl.ds(256, 256)
    more = [
        remote(fin.at[1 - core, :, lo], all_ref.at[1, :, my_cols], out_s.at[1], out_r.at[1], sib),
        remote(fin.at[1 - core, :, hi], all_ref.at[2, :, my_cols], out_s.at[2], out_r.at[2], sib),
        local(fin.at[core, :, lo], all_ref.at[1, :, my_cols], out_l.at[1]),
        local(fin.at[core, :, hi], all_ref.at[2, :, my_cols], out_l.at[2]),
    ]

    def finish():
        for b, copies in ((1 - core, more[:2]), (core, more[2:])):
            pick = jnp.where(g0 == b0 + b, 1.0, 0.0).astype(F32)
            fin[b] = (own[b] + gs0[...].astype(F32) * pick).astype(BF)
            for cp in copies:
                cp.start()

    @pl.when(chip != 31)
    def _():
        finish()

    @pl.when(chip == 31)
    def _():
        local(hsum.at[1], piece(gs63, z, y), gs_r.at[1]).start()
        wait(gs63, gs_r.at[1])
        own[1] += gs63[...].astype(F32)
        finish()

    for cp in pairs:
        cp.wait_send()
    for cp in nbk:
        cp.wait_send()
    for cp in nbg:
        cp.wait_send()

    @pl.when(chip == 31)
    def _():
        wait(rsel.at[pl.ds(0, 31)], sc_s)

    @pl.when(chip != 31)
    def _():
        wait(hsum.at[1], gs_s.at[1])

    wait(rsel.at[pl.ds(0, 31)], sel_s)
    wait(rsel.at[pl.ds(0, 30)], do_s)
    wait(rsel.at[pl.ds(0, 31)], ag_s.at[0])
    wait(rsel.at[pl.ds(0, 31)], ag_s.at[1])
    wait(rsel.at[pl.ds(0, 31)], rg_s.at[0])
    wait(rsel.at[pl.ds(0, 31)], rg_s.at[1])
    wait(rsel.at[pl.ds(0, 31)], gs_s.at[0])
    for cp in outs + more:
        cp.wait()


def shards(queries, key_states, values, out_grad, pattern, global_ids):
    vmem = pltpu.VMEM
    dma = pltpu.SemaphoreType.DMA
    hbm = pl.BlockSpec(memory_space=pltpu.HBM)
    anyspace = pl.BlockSpec(memory_space=pl.ANY)
    smem = pl.BlockSpec(memory_space=pltpu.SMEM)
    out = jax.ShapeDtypeStruct((3, BLK, 512), BF)
    operands = (pattern.T, global_ids, queries, key_states, values, out_grad)
    grads = pl.pallas_call(
        kernel,
        out_shape=out,
        in_specs=[hbm] * 6,
        out_specs=anyspace,
        scratch_shapes=[
            pltpu.SMEM((3, 64), jnp.int32),
            pltpu.SMEM((2,), jnp.int32),
            vmem((2, BLK, 256), BF),
            vmem((2, BLK, 512), BF),
            vmem((2, BLK, 512), BF),
            vmem((2, BLK, 256), BF),
            vmem((BLK, 512), BF),
            vmem((32, 16, 128), BF),
            vmem((2, 16, 128), BF),
            vmem((2, BLK, 512), BF),
            vmem((2, BLK, 512), BF),
            vmem((2, 32, 16, 128), BF),
            vmem((2, 16, 128), BF),
            vmem((BLK, 512), BF),
            vmem((BLK, 512), BF),
            vmem((2, 2, BLK, 256), BF),
            vmem((2, 2, BLK, 256), BF),
            vmem((2, BLK, 512), F32),
            vmem((2, BLK, 512), BF),
            vmem((2, BLK, 256), BF),
            vmem((2, 384, 256), F32),
            vmem((2, 384, 256), F32),
            vmem((2, 256, 256), BF),
            pltpu.SemaphoreType.REGULAR, pltpu.SemaphoreType.REGULAR, pltpu.SemaphoreType.REGULAR((32,)),
            dma((5,)),
            dma((3,)), dma((3,)),
            dma((2,)), dma((2,)),
            dma, dma,
            dma, dma,
            dma, dma,
            dma((2,)), dma((2,)),
            dma((2,)), dma((2,)),
            dma((2,)), dma((2,)),
            dma((2, 2)), dma((2, 2)),
            dma((3,)), dma((3,)), dma((3,)),
        ],
        name="block_attention_grads",
        compiler_params=pltpu.CompilerParams(
            collective_id=0, has_side_effects=True, vmem_limit_bytes=32 * 1024 * 1024
        ),
    )(*[pltpu.with_memory_space_constraint(a, pltpu.HBM) for a in operands])
    return grads[0], grads[1], grads[2]


def solution(mesh):
    placed = (
        P("ctx", "head"),
        P("ctx", "head"),
        P("ctx", "head"),
        P(("ctx", "head"), None),
        P(),
        P(),
    )
    return jax.shard_map(
        shards,
        mesh=mesh,
        in_specs=placed,
        out_specs=(P("ctx", "head"), P("ctx", "head"), P("ctx", "head")),
        check_vma=False,
    )
```
